32 devices in a mesh: groups: 2 (over y), seq: 4 (over z), head: 4 (over x, core).
Axes of the slice: x: 2, y: 2, z: 4, core: 2. Of those that a mesh axis runs over, the one named last changes fastest.
Arguments:
- query: bfloat16 [16, 1024, 128], P('head', ('groups', 'seq')), parts along dimension 1, may hold values from -400 to 400
- keys: bfloat16 [4, 1024, 128], P('head', ('groups', 'seq')), parts along dimension 1, may hold values from -5 to 5
- values: bfloat16 [4, 1024, 128], P('head', ('groups', 'seq')), parts along dimension 1, may hold values from -6 to 6
- ratio: bfloat16 [16, 1024, 128], P('head', ('groups', 'seq')), parts along dimension 1, may hold values from -4 to 4
- block_order: int32 [16], P('groups'), parts along dimension 0, may hold values from 0 to 7, each once
Outputs:
- query_rel: float32 [16, 1024, 128], P('head', ('groups', 'seq')), parts along dimension 1
- key_rel: float32 [4, 1024, 128], P('head', ('groups', 'seq')), parts along dimension 1
- value_rel: float32 [4, 1024, 128], P('head', ('groups', 'seq')), parts along dimension 1
The draws below stay inside these ranges and needn't reach their ends.
There are 2 independent parts, one for each index of `groups`. The reference program is written for one: setup_inputs(seed, part) draws one part's arguments, and reference() takes and returns one part's arrays. A program takes and returns all parts, laid end to end along the dimension named above; each array names one. Nothing has to cross between parts.
Inputs may be any that keep to these rules, and one draw needn't show every extreme that they name: A permutation: stored block b holds prompt block block_order[b], each once.
All inputs are finite; a program needn't handle non-finite values.
Results may differ from the reference program's by a relative error of at most 0.04.
Values may be sent and summed in bfloat16 or wider, within the bound.
A program may use at most 64 MiB of HBM per device.

```python
import jax
import jax.numpy as jnp
from jax import lax

HD = 128
QPK = 4
KVH = 4
QH = 16
TOKENS = 512
BLK = 64
NBLK = 8


def query_and_keys(key):
    base = jax.random.fold_in(key, 11)
    first_key, second_key = jax.random.split(base, 2)
    keys = jnp.clip(jax.random.normal(first_key, (KVH, TOKENS, HD), jnp.float32), -4.0, 4.0)
    query = jnp.clip(jax.random.normal(second_key, (QH, TOKENS, HD), jnp.float32), -4.0, 4.0)
    return (query, keys)


def draw_query(key, part):
    return query_and_keys(key)[0].astype(jnp.bfloat16)


def draw_keys(key, part):
    return query_and_keys(key)[1].astype(jnp.bfloat16)


def shard_levels(own_key, dims, pieces, least, top_value):
    level = 1.0
    for dim, parts in pieces:
        draws = jax.random.uniform(jax.random.fold_in(jax.random.fold_in(own_key, 6), dim), (parts,), jnp.float32, least / len(pieces), top_value / len(pieces))
        level = level * jnp.repeat(jnp.exp(draws), dims[dim] // parts).reshape((-1,) + (1,) * (len(dims) - 1 - dim))
    return level


def normal_values(own_key, shape, scale, limit, shards=(), kind=jnp.bfloat16):
    level = shard_levels(own_key, shape, shards, -0.22, 0.18) if shards else 1.0
    array = jax.random.normal(own_key, shape, jnp.float32) * scale * level
    return jnp.minimum(jnp.maximum(array, -limit), limit).astype(kind)


def setup_inputs(seed: int = 0, part: int = 0) -> dict:
    seeds = jax.random.split(jax.random.key(seed), 6)
    part_splits = jax.random.split(jax.random.fold_in(seeds[5], part), 6)
    return {
        "query": draw_query(jax.random.fold_in(jax.random.fold_in(seeds[5], part), 71), part),
        "keys": draw_keys(jax.random.fold_in(jax.random.fold_in(seeds[5], part), 71), part),
        "values": normal_values(part_splits[2], (KVH, TOKENS, HD), 1.0, 6.0, ((0, 4), (1, 4))),
        "ratio": normal_values(part_splits[3], (QH, TOKENS, HD), 0.5, 4.0, ((0, 4), (1, 4))),
        "block_order": jax.random.permutation(part_splits[4], NBLK).astype(jnp.int32),
    }


def token_places(block_order):
    offsets = jnp.arange(BLK, dtype=jnp.int32)
    return (block_order[:, None] * BLK + offsets[None, :]).reshape(-1)


def reference(query, keys, values, ratio, block_order):
    score_scale = HD ** -0.5
    places = token_places(block_order)
    visible = places[None, :] <= places[:, None]
    grouped_query = query.reshape(KVH, QPK, TOKENS, HD)
    grouped_ratio = ratio.reshape(KVH, QPK, TOKENS, HD)

    def one_group(operands):
        query_heads, ratio_heads, key_rows, value_rows = operands

        def one_head(head_pair):
            query_rows, ratio_rows = head_pair
            scores = jnp.dot(query_rows, key_rows.T, preferred_element_type=jnp.float32) * score_scale
            scores = jnp.where(visible, scores, -jnp.inf)
            row_top = jnp.max(scores, axis=1, keepdims=True)
            exp_scores = jnp.exp(scores - row_top)
            weights = exp_scores / jnp.sum(exp_scores, axis=1, keepdims=True)
            prob_grad = jnp.dot(ratio_rows, value_rows.T, preferred_element_type=jnp.float32)
            row_expect = jnp.sum(weights * prob_grad, axis=1, keepdims=True)
            soft_grad = (weights * (prob_grad - row_expect)).astype(jnp.bfloat16)
            low_weights = weights.astype(jnp.bfloat16)
            query_part = 0.5 * score_scale * query_rows.astype(jnp.float32) * jnp.dot(soft_grad, key_rows, preferred_element_type=jnp.float32)
            key_part = jnp.dot(soft_grad.T, query_rows, preferred_element_type=jnp.float32)
            value_part = jnp.dot(low_weights.T, ratio_rows, preferred_element_type=jnp.float32)
            return query_part, key_part, value_part

        query_part, key_part, value_part = lax.map(one_head, (query_heads, ratio_heads))
        key_out = 0.5 * score_scale * key_rows.astype(jnp.float32) * jnp.sum(key_part, axis=0)
        value_out = value_rows.astype(jnp.float32) * jnp.sum(value_part, axis=0)
        return query_part, key_out, value_out

    query_rel, key_rel, value_rel = lax.map(one_group, (grouped_query, grouped_ratio, keys, values))
    return query_rel.reshape(QH, TOKENS, HD), key_rel, value_rel
```

```python
import functools
import math

import jax
import jax.numpy as jnp
from jax import lax
from jax.experimental import pallas as pl
from jax.experimental.pallas import tpu as pltpu
from jax.sharding import PartitionSpec as P

MESH = pl.DeviceIdType.MESH
MASKED = -1e30
NT = (((1,), (1,)), ((), ()))
TN = (((0,), (0,)), ((), ()))


def dot(a, b, dims=None):
    if dims is None:
        return jnp.dot(a, b, preferred_element_type=jnp.float32)
    return lax.dot_general(a, b, dims, preferred_element_type=jnp.float32)


def each(first, last, step):
    if last - first <= 8:
        for i in range(first, last):
            step(i)
    else:
        pl.loop(first, last)(step)


def kernel(
    n,
    order_ref,
    query_hbm,
    keys_hbm,
    values_hbm,
    ratio_hbm,
    query_rel,
    key_rel,
    value_rel,
    query,
    ratio,
    kbuf,
    vbuf,
    exps,
    grads,
    tops,
    sums,
    low,
    soft,
    dv_out,
    dk_out,
    dv_in,
    dk_in,
    local_sem,
    k_send,
    k_recv,
    v_send,
    v_recv,
    dv_send,
    dv_recv,
    dk_send,
    dk_recv,
):
    heads, rows, depth = query_hbm.shape
    wide = heads * rows
    scale = depth**-0.5
    rate = scale * math.log2(math.e)
    per_device = order_ref.shape[0] // n
    block_rows = rows // per_device
    me = lax.axis_index("seq")

    def to(d):
        return {"seq": lax.rem(me + d, n)}

    def back(d):
        return {"seq": lax.rem(me + n - d, n)}

    loads = [
        pltpu.make_async_copy(keys_hbm.at[0], kbuf.at[0], local_sem.at[0]),
        pltpu.make_async_copy(query_hbm, query, local_sem.at[1]),
        pltpu.make_async_copy(ratio_hbm, ratio, local_sem.at[2]),
        pltpu.make_async_copy(values_hbm.at[0], vbuf.at[0], local_sem.at[3]),
    ]
    for load in loads:
        load.start()

    barrier = pltpu.get_barrier_semaphore()

    def greet(d):
        pl.semaphore_signal(barrier, inc=1, device_id=to(d), device_id_type=MESH)

    each(1, n, greet)
    pl.semaphore_wait(barrier, n - 1)

    def k_copy(d):
        return pltpu.make_async_remote_copy(
            src_ref=keys_hbm.at[0],
            dst_ref=kbuf.at[d],
            send_sem=k_send.at[d],
            recv_sem=k_recv.at[d],
            device_id=to(d),
            device_id_type=MESH,
        )

    def v_copy(d):
        return pltpu.make_async_remote_copy(
            src_ref=values_hbm.at[0],
            dst_ref=vbuf.at[d],
            send_sem=v_send.at[d],
            recv_sem=v_recv.at[d],
            device_id=to(d),
            device_id_type=MESH,
        )

    def dv_copy(d):
        return pltpu.make_async_remote_copy(
            src_ref=dv_out.at[d],
            dst_ref=dv_in.at[d],
            send_sem=dv_send.at[d],
            recv_sem=dv_recv.at[d],
            device_id=back(d),
            device_id_type=MESH,
        )

    def dk_copy(d):
        return pltpu.make_async_remote_copy(
            src_ref=dk_out.at[d],
            dst_ref=dk_in.at[d],
            send_sem=dk_send.at[d],
            recv_sem=dk_recv.at[d],
            device_id=back(d),
            device_id_type=MESH,
        )

    each(1, n, lambda d: k_copy(d).start())
    each(1, n, lambda d: v_copy(d).start())

    def places(owner, axis):
        index = lax.broadcasted_iota(jnp.int32, (rows, rows), axis)
        within = lax.rem(index, block_rows)
        first = order_ref[owner * per_device] * block_rows
        for b in range(1, per_device):
            first = jnp.where(
                index >= b * block_rows, order_ref[owner * per_device + b] * block_rows, first
            )
        return first + within

    loads[0].wait()
    loads[1].wait()
    query_places = places(me, 1)

    def score_step(d):
        owner = lax.rem(me + n - d, n)
        bias = jnp.where(places(owner, 0) <= query_places, 0.0, MASKED)
        rows_in = query[...].reshape(wide, depth)
        scores = dot(kbuf[d], rows_in, NT) + jnp.concatenate([bias] * heads, axis=1)
        top = jnp.max(scores, axis=0, keepdims=True)
        e = jnp.exp2((scores - top) * rate)
        exps[d] = e
        tops[d] = top
        sums[d] = jnp.sum(e, axis=0, keepdims=True)

    score_step(0)
    loads[2].wait()
    loads[3].wait()

    def grad_step(d):
        grads[d] = dot(vbuf[d], ratio[...].reshape(wide, depth), NT)

    grad_step(0)

    def k_step(d):
        k_copy(d).wait_recv()
        score_step(d)

    each(1, n, k_step)

    top = jnp.max(tops[...], axis=0)
    total = jnp.sum(sums[...] * jnp.exp2((tops[...] - top) * rate), axis=0)
    inverse = 1.0 / total

    def weight_step(d):
        w = exps[d] * (jnp.exp2((tops[d] - top) * rate) * inverse)
        exps[d] = w
        low[d] = w.astype(jnp.bfloat16)

    def value_part(d):
        return dot(low[d], ratio[...].reshape(wide, depth))

    def dv_step(d):
        weight_step(d)
        dv_out[d] = value_part(d).astype(jnp.bfloat16)
        dv_copy(d).start()

    each(1, n, dv_step)
    weight_step(0)
    own_value = value_part(0)

    def v_step(d):
        v_copy(d).wait_recv()
        grad_step(d)

    each(1, n, v_step)

    if n <= 8:
        expect = sum(jnp.sum(exps[d] * grads[d], axis=0, keepdims=True) for d in range(n))
    else:
        expect = lax.fori_loop(
            0,
            n,
            lambda d, e: e + jnp.sum(exps[d] * grads[d], axis=0, keepdims=True),
            jnp.zeros((1, wide), jnp.float32),
        )

    def soft_step(d):
        soft[d] = (exps[d] * (grads[d] - expect)).astype(jnp.bfloat16)

    def key_part(d):
        return dot(soft[d], query[...].reshape(wide, depth))

    def dk_step(d):
        soft_step(d)
        dk_out[d] = key_part(d).astype(jnp.bfloat16)
        dk_copy(d).start()

    each(1, n, dk_step)
    soft_step(0)
    own_key = key_part(0)

    query_sum = dot(
        kbuf[...].reshape(n * rows, depth), soft[...].reshape(n * rows, wide), TN
    )
    for h in range(heads):
        query_rel[h] = (
            0.5
            * scale
            * query[h].astype(jnp.float32)
            * query_sum[:, h * rows : (h + 1) * rows].T
        )

    each(1, n, lambda d: dv_copy(d).wait_recv())
    value_rel[0] = vbuf[0].astype(jnp.float32) * (
        own_value + jnp.sum(dv_in[1:].astype(jnp.float32), axis=0)
    )
    each(1, n, lambda d: dk_copy(d).wait_recv())
    key_rel[0] = (
        0.5
        * scale
        * kbuf[0].astype(jnp.float32)
        * (own_key + jnp.sum(dk_in[1:].astype(jnp.float32), axis=0))
    )

    def drain(d):
        k_copy(d).wait_send()
        v_copy(d).wait_send()
        dv_copy(d).wait_send()
        dk_copy(d).wait_send()

    each(1, n, drain)


def body(n, query, keys, values, ratio, block_order):
    heads, rows, depth = query.shape
    wide = heads * rows
    bf16, f32 = jnp.bfloat16, jnp.float32
    anywhere = pl.BlockSpec(memory_space=pl.ANY)
    vmem = pl.BlockSpec(memory_space=pltpu.VMEM)
    dma = pltpu.SemaphoreType.DMA((n,))
    return pl.pallas_call(
        functools.partial(kernel, n),
        out_shape=[
            jax.ShapeDtypeStruct(query.shape, f32),
            jax.ShapeDtypeStruct(keys.shape, f32),
            jax.ShapeDtypeStruct(values.shape, f32),
        ],
        in_specs=[pl.BlockSpec(memory_space=pltpu.SMEM)] + [anywhere] * 4,
        out_specs=[vmem] * 3,
        scratch_shapes=[
            pltpu.VMEM((heads, rows, depth), bf16),
            pltpu.VMEM((heads, rows, depth), bf16),
            pltpu.VMEM((n, rows, depth), bf16),
            pltpu.VMEM((n, rows, depth), bf16),
            pltpu.VMEM((n, rows, wide), f32),
            pltpu.VMEM((n, rows, wide), f32),
            pltpu.VMEM((n, 1, wide), f32),
            pltpu.VMEM((n, 1, wide), f32),
            pltpu.VMEM((n, rows, wide), bf16),
            pltpu.VMEM((n, rows, wide), bf16),
            pltpu.VMEM((n, rows, depth), bf16),
            pltpu.VMEM((n, rows, depth), bf16),
            pltpu.VMEM((n, rows, depth), bf16),
            pltpu.VMEM((n, rows, depth), bf16),
            pltpu.SemaphoreType.DMA((4,)),
        ]
        + [dma] * 8,
        compiler_params=pltpu.CompilerParams(
            collective_id=0, has_side_effects=True, vmem_limit_bytes=56 * 2**20
        ),
    )(block_order, query, keys, values, ratio)


def solution(mesh):
    spec = P("head", ("groups", "seq"), None)
    return jax.shard_map(
        functools.partial(body, mesh.shape["seq"]),
        mesh=mesh,
        in_specs=(spec, spec, spec, spec, P("groups")),
        out_specs=(spec, spec, spec),
        check_vma=False,
    )
```

```python
import functools
import math

import jax
import jax.numpy as jnp
from jax import lax
from jax.experimental import pallas as pl
from jax.experimental.pallas import tpu as pltpu
from jax.sharding import PartitionSpec as P

MESH = pl.DeviceIdType.MESH
MASKED = -1e30
NT = (((1,), (1,)), ((), ()))
TN = (((0,), (0,)), ((), ()))


def dot(a, b, dims=None):
    if dims is None:
        return jnp.dot(a, b, preferred_element_type=jnp.float32)
    return lax.dot_general(a, b, dims, preferred_element_type=jnp.float32)


def each(first, last, step):
    if last - first <= 8:
        for i in range(first, last):
            step(i)
    else:
        pl.loop(first, last)(step)


def kernel(
    n,
    order_ref,
    query_hbm,
    keys_hbm,
    values_hbm,
    ratio_hbm,
    query_rel,
    key_rel,
    value_rel,
    query,
    ratio,
    kbuf,
    vbuf,
    exps,
    grads,
    tops,
    sums,
    low,
    soft,
    dv_out,
    dk_out,
    dv_in,
    dk_in,
    local_sem,
    k_send,
    k_recv,
    v_send,
    v_recv,
    dv_send,
    dv_recv,
    dk_send,
    dk_recv,
):
    heads, rows, depth = query_hbm.shape
    wide = heads * rows
    scale = depth**-0.5
    rate = scale * math.log2(math.e)
    per_device = order_ref.shape[0] // n
    block_rows = rows // per_device
    me = lax.axis_index("seq")

    def to(d):
        return {"seq": lax.rem(me + d, n)}

    def back(d):
        return {"seq": lax.rem(me + n - d, n)}

    loads = [
        pltpu.make_async_copy(keys_hbm.at[0], kbuf.at[0], local_sem.at[0]),
        pltpu.make_async_copy(query_hbm, query, local_sem.at[1]),
        pltpu.make_async_copy(ratio_hbm, ratio, local_sem.at[2]),
        pltpu.make_async_copy(values_hbm.at[0], vbuf.at[0], local_sem.at[3]),
    ]
    for load in loads:
        load.start()

    barrier = pltpu.get_barrier_semaphore()

    def greet(d):
        pl.semaphore_signal(barrier, inc=1, device_id=to(d), device_id_type=MESH)

    each(1, n, greet)
    pl.semaphore_wait(barrier, n - 1)

    def k_copy(d):
        return pltpu.make_async_remote_copy(
            src_ref=keys_hbm.at[0],
            dst_ref=kbuf.at[d],
            send_sem=k_send.at[d],
            recv_sem=k_recv.at[d],
            device_id=to(d),
            device_id_type=MESH,
        )

    def v_copy(d):
        return pltpu.make_async_remote_copy(
            src_ref=values_hbm.at[0],
            dst_ref=vbuf.at[d],
            send_sem=v_send.at[d],
            recv_sem=v_recv.at[d],
            device_id=to(d),
            device_id_type=MESH,
        )

    def dv_copy(d):
        return pltpu.make_async_remote_copy(
            src_ref=dv_out.at[d],
            dst_ref=dv_in.at[d],
            send_sem=dv_send.at[d],
            recv_sem=dv_recv.at[d],
            device_id=back(d),
            device_id_type=MESH,
        )

    def dk_copy(d):
        return pltpu.make_async_remote_copy(
            src_ref=dk_out.at[d],
            dst_ref=dk_in.at[d],
            send_sem=dk_send.at[d],
            recv_sem=dk_recv.at[d],
            device_id=back(d),
            device_id_type=MESH,
        )

    each(1, n, lambda d: k_copy(d).start())
    each(1, n, lambda d: v_copy(d).start())

    def places(owner, axis):
        index = lax.broadcasted_iota(jnp.int32, (rows, rows), axis)
        within = lax.rem(index, block_rows)
        first = order_ref[owner * per_device] * block_rows
        for b in range(1, per_device):
            first = jnp.where(
                index >= b * block_rows, order_ref[owner * per_device + b] * block_rows, first
            )
        return first + within

    loads[0].wait()
    loads[1].wait()
    query_places = places(me, 1)

    def score_step(d):
        owner = lax.rem(me + n - d, n)
        bias = jnp.where(places(owner, 0) <= query_places, 0.0, MASKED)
        rows_in = query[...].reshape(wide, depth)
        scores = dot(kbuf[d], rows_in, NT) + jnp.concatenate([bias] * heads, axis=1)
        top = jnp.max(scores, axis=0, keepdims=True)
        e = jnp.exp2((scores - top) * rate)
        exps[d] = e
        tops[d] = top
        sums[d] = jnp.sum(e, axis=0, keepdims=True)

    score_step(0)
    loads[2].wait()
    loads[3].wait()

    def grad_step(d):
        grads[d] = dot(vbuf[d], ratio[...].reshape(wide, depth), NT)

    grad_step(0)

    def k_step(d):
        k_copy(d).wait_recv()
        score_step(d)

    each(1, n, k_step)

    top = jnp.max(tops[...], axis=0)
    total = jnp.sum(sums[...] * jnp.exp2((tops[...] - top) * rate), axis=0)
    inverse = 1.0 / total

    def weight_step(d):
        w = exps[d] * (jnp.exp2((tops[d] - top) * rate) * inverse)
        exps[d] = w
        low[d] = w.astype(jnp.bfloat16)

    def value_part(d):
        return dot(low[d], ratio[...].reshape(wide, depth))

    def dv_step(d):
        weight_step(d)
        dv_out[d] = value_part(d).astype(jnp.bfloat16)
        dv_copy(d).start()

    each(1, n, dv_step)
    weight_step(0)
    own_value = value_part(0)

    def v_step(d):
        v_copy(d).wait_recv()
        grad_step(d)

    each(1, n, v_step)

    if n <= 8:
        expect = sum(jnp.sum(exps[d] * grads[d], axis=0, keepdims=True) for d in range(n))
    else:
        expect = lax.fori_loop(
            0,
            n,
            lambda d, e: e + jnp.sum(exps[d] * grads[d], axis=0, keepdims=True),
            jnp.zeros((1, wide), jnp.float32),
        )

    def soft_step(d):
        soft[d] = (exps[d] * (grads[d] - expect)).astype(jnp.bfloat16)

    def key_part(d):
        return dot(soft[d], query[...].reshape(wide, depth))

    def dk_step(d):
        soft_step(d)
        dk_out[d] = key_part(d).astype(jnp.bfloat16)
        dk_copy(d).start()

    each(1, n, dk_step)
    soft_step(0)
    own_key = key_part(0)

    query_sum = dot(
        kbuf[...].reshape(n * rows, depth), soft[...].reshape(n * rows, wide), TN
    )
    for h in range(heads):
        query_rel[h] = (
            0.5
            * scale
            * query[h].astype(jnp.float32)
            * query_sum[:, h * rows : (h + 1) * rows].T
        )

    each(1, n, lambda d: dv_copy(d).wait_recv())
    value_rel[0] = vbuf[0].astype(jnp.float32) * (
        own_value + jnp.sum(dv_in[1:].astype(jnp.float32), axis=0)
    )
    each(1, n, lambda d: dk_copy(d).wait_recv())
    key_rel[0] = (
        0.5
        * scale
        * kbuf[0].astype(jnp.float32)
        * (own_key + jnp.sum(dk_in[1:].astype(jnp.float32), axis=0))
    )

    def drain(d):
        k_copy(d).wait_send()
        v_copy(d).wait_send()
        dv_copy(d).wait_send()
        dk_copy(d).wait_send()

    each(1, n, drain)


def body(n, query, keys, values, ratio, block_order):
    heads, rows, depth = query.shape
    wide = heads * rows
    bf16, f32 = jnp.bfloat16, jnp.float32
    anywhere = pl.BlockSpec(memory_space=pl.ANY)
    vmem = pl.BlockSpec(memory_space=pltpu.VMEM)
    dma = pltpu.SemaphoreType.DMA((n,))
    return pl.pallas_call(
        functools.partial(kernel, n),
        out_shape=[
            pltpu.VMEM(query.shape, f32),
            pltpu.VMEM(keys.shape, f32),
            pltpu.VMEM(values.shape, f32),
        ],
        in_specs=[pl.BlockSpec(memory_space=pltpu.SMEM)] + [anywhere] * 4,
        out_specs=[vmem] * 3,
        scratch_shapes=[
            pltpu.VMEM((heads, rows, depth), bf16),
            pltpu.VMEM((heads, rows, depth), bf16),
            pltpu.VMEM((n, rows, depth), bf16),
            pltpu.VMEM((n, rows, depth), bf16),
            pltpu.VMEM((n, rows, wide), f32),
            pltpu.VMEM((n, rows, wide), f32),
            pltpu.VMEM((n, 1, wide), f32),
            pltpu.VMEM((n, 1, wide), f32),
            pltpu.VMEM((n, rows, wide), bf16),
            pltpu.VMEM((n, rows, wide), bf16),
            pltpu.VMEM((n, rows, depth), bf16),
            pltpu.VMEM((n, rows, depth), bf16),
            pltpu.VMEM((n, rows, depth), bf16),
            pltpu.VMEM((n, rows, depth), bf16),
            pltpu.SemaphoreType.DMA((4,)),
        ]
        + [dma] * 8,
        compiler_params=pltpu.CompilerParams(
            collective_id=0, has_side_effects=True, vmem_limit_bytes=56 * 2**20
        ),
    )(block_order, query, keys, values, ratio)


def solution(mesh):
    spec = P("head", ("groups", "seq"), None)
    return jax.shard_map(
        functools.partial(body, mesh.shape["seq"]),
        mesh=mesh,
        in_specs=(spec, spec, spec, spec, P("groups")),
        out_specs=(spec, spec, spec),
        check_vma=False,
    )
```

```python
import functools
import math

import jax
import jax.numpy as jnp
from jax import lax
from jax.experimental import pallas as pl
from jax.experimental.pallas import tpu as pltpu
from jax.sharding import PartitionSpec as P

MESH = pl.DeviceIdType.MESH
MASKED = -1e30
NT = (((1,), (1,)), ((), ()))
TN = (((0,), (0,)), ((), ()))


def dot(a, b, dims=None):
    if dims is None:
        return jnp.dot(a, b, preferred_element_type=jnp.float32)
    return lax.dot_general(a, b, dims, preferred_element_type=jnp.float32)


def each(first, last, step):
    if last - first <= 8:
        for i in range(first, last):
            step(i)
    else:
        pl.loop(first, last)(step)


def kernel(
    n,
    order_ref,
    query_hbm,
    keys_hbm,
    values_hbm,
    ratio_hbm,
    query_rel,
    key_rel,
    value_rel,
    query,
    ratio,
    kbuf,
    vbuf,
    exps,
    grads,
    tops,
    sums,
    low,
    soft,
    dv_out,
    dk_out,
    dv_in,
    dk_in,
    local_sem,
    k_send,
    k_recv,
    v_send,
    v_recv,
    dv_send,
    dv_recv,
    dk_send,
    dk_recv,
):
    heads, rows, depth = query_hbm.shape
    wide = heads * rows
    scale = depth**-0.5
    rate = scale * math.log2(math.e)
    per_device = order_ref.shape[0] // n
    block_rows = rows // per_device
    me = lax.axis_index("seq")

    pair = me + 1 - 2 * lax.rem(me, 2)

    def peer(d, sign):
        odd = d % 2
        return lax.rem(me + (pair - me) * odd + n + sign * (d - odd), n)

    def to(d):
        return {"seq": peer(d, 1)}

    def back(d):
        return {"seq": peer(d, -1)}

    def each_peer(step):
        each(2, n, step)
        step(1)

    loads = [
        pltpu.make_async_copy(keys_hbm.at[0], kbuf.at[0], local_sem.at[0]),
        pltpu.make_async_copy(query_hbm, query, local_sem.at[1]),
        pltpu.make_async_copy(ratio_hbm, ratio, local_sem.at[2]),
        pltpu.make_async_copy(values_hbm.at[0], vbuf.at[0], local_sem.at[3]),
    ]
    for load in loads:
        load.start()

    barrier = pltpu.get_barrier_semaphore()

    def greet(d):
        pl.semaphore_signal(barrier, inc=1, device_id=to(d), device_id_type=MESH)

    each(1, n, greet)
    pl.semaphore_wait(barrier, n - 1)

    def k_copy(d):
        return pltpu.make_async_remote_copy(
            src_ref=keys_hbm.at[0],
            dst_ref=kbuf.at[d],
            send_sem=k_send.at[d],
            recv_sem=k_recv.at[d],
            device_id=to(d),
            device_id_type=MESH,
        )

    def v_copy(d):
        return pltpu.make_async_remote_copy(
            src_ref=values_hbm.at[0],
            dst_ref=vbuf.at[d],
            send_sem=v_send.at[d],
            recv_sem=v_recv.at[d],
            device_id=to(d),
            device_id_type=MESH,
        )

    def dv_copy(d):
        return pltpu.make_async_remote_copy(
            src_ref=dv_out.at[d],
            dst_ref=dv_in.at[d],
            send_sem=dv_send.at[d],
            recv_sem=dv_recv.at[d],
            device_id=back(d),
            device_id_type=MESH,
        )

    def dk_copy(d):
        return pltpu.make_async_remote_copy(
            src_ref=dk_out.at[d],
            dst_ref=dk_in.at[d],
            send_sem=dk_send.at[d],
            recv_sem=dk_recv.at[d],
            device_id=back(d),
            device_id_type=MESH,
        )

    each_peer(lambda d: k_copy(d).start())
    each_peer(lambda d: v_copy(d).start())

    def places(owner, axis):
        index = lax.broadcasted_iota(jnp.int32, (rows, rows), axis)
        within = lax.rem(index, block_rows)
        first = order_ref[owner * per_device] * block_rows
        for b in range(1, per_device):
            first = jnp.where(
                index >= b * block_rows, order_ref[owner * per_device + b] * block_rows, first
            )
        return first + within

    loads[0].wait()
    loads[1].wait()
    query_places = places(me, 1)

    def score_step(d):
        owner = peer(d, -1)
        bias = jnp.where(places(owner, 0) <= query_places, 0.0, MASKED)
        rows_in = query[...].reshape(wide, depth)
        scores = dot(kbuf[d], rows_in, NT) + jnp.concatenate([bias] * heads, axis=1)
        top = jnp.max(scores, axis=0, keepdims=True)
        e = jnp.exp2((scores - top) * rate)
        exps[d] = e
        tops[d] = top
        sums[d] = jnp.sum(e, axis=0, keepdims=True)

    score_step(0)
    loads[2].wait()
    loads[3].wait()

    def grad_step(d):
        grads[d] = dot(vbuf[d], ratio[...].reshape(wide, depth), NT)

    grad_step(0)

    def k_step(d):
        k_copy(d).wait_recv()
        score_step(d)

    each(1, n, k_step)

    top = jnp.max(tops[...], axis=0)
    total = jnp.sum(sums[...] * jnp.exp2((tops[...] - top) * rate), axis=0)
    inverse = 1.0 / total

    def weight_step(d):
        w = exps[d] * (jnp.exp2((tops[d] - top) * rate) * inverse)
        exps[d] = w
        low[d] = w.astype(jnp.bfloat16)

    def value_part(d):
        return dot(low[d], ratio[...].reshape(wide, depth))

    def dv_step(d):
        weight_step(d)
        dv_out[d] = value_part(d).astype(jnp.bfloat16)
        dv_copy(d).start()

    each(1, n, dv_step)
    weight_step(0)
    own_value = value_part(0)

    def v_step(d):
        v_copy(d).wait_recv()
        grad_step(d)

    each(1, n, v_step)

    if n <= 8:
        expect = sum(jnp.sum(exps[d] * grads[d], axis=0, keepdims=True) for d in range(n))
    else:
        expect = lax.fori_loop(
            0,
            n,
            lambda d, e: e + jnp.sum(exps[d] * grads[d], axis=0, keepdims=True),
            jnp.zeros((1, wide), jnp.float32),
        )

    def soft_step(d):
        soft[d] = (exps[d] * (grads[d] - expect)).astype(jnp.bfloat16)

    def key_part(d):
        return dot(soft[d], query[...].reshape(wide, depth))

    def dk_step(d):
        soft_step(d)
        dk_out[d] = key_part(d).astype(jnp.bfloat16)
        dk_copy(d).start()

    each(1, n, dk_step)
    soft_step(0)
    own_key = key_part(0)

    query_sum = dot(
        kbuf[...].reshape(n * rows, depth), soft[...].reshape(n * rows, wide), TN
    )
    for h in range(heads):
        query_rel[h] = (
            0.5
            * scale
            * query[h].astype(jnp.float32)
            * query_sum[:, h * rows : (h + 1) * rows].T
        )

    each(1, n, lambda d: dv_copy(d).wait_recv())
    value_rel[0] = vbuf[0].astype(jnp.float32) * (
        own_value + jnp.sum(dv_in[1:].astype(jnp.float32), axis=0)
    )
    each(1, n, lambda d: dk_copy(d).wait_recv())
    key_rel[0] = (
        0.5
        * scale
        * kbuf[0].astype(jnp.float32)
        * (own_key + jnp.sum(dk_in[1:].astype(jnp.float32), axis=0))
    )

    def drain(d):
        k_copy(d).wait_send()
        v_copy(d).wait_send()
        dv_copy(d).wait_send()
        dk_copy(d).wait_send()

    each(1, n, drain)


def body(n, query, keys, values, ratio, block_order):
    heads, rows, depth = query.shape
    wide = heads * rows
    bf16, f32 = jnp.bfloat16, jnp.float32
    anywhere = pl.BlockSpec(memory_space=pl.ANY)
    vmem = pl.BlockSpec(memory_space=pltpu.VMEM)
    dma = pltpu.SemaphoreType.DMA((n,))
    return pl.pallas_call(
        functools.partial(kernel, n),
        out_shape=[
            pltpu.VMEM(query.shape, f32),
            pltpu.VMEM(keys.shape, f32),
            pltpu.VMEM(values.shape, f32),
        ],
        in_specs=[pl.BlockSpec(memory_space=pltpu.SMEM)] + [anywhere] * 4,
        out_specs=[vmem] * 3,
        scratch_shapes=[
            pltpu.VMEM((heads, rows, depth), bf16),
            pltpu.VMEM((heads, rows, depth), bf16),
            pltpu.VMEM((n, rows, depth), bf16),
            pltpu.VMEM((n, rows, depth), bf16),
            pltpu.VMEM((n, rows, wide), f32),
            pltpu.VMEM((n, rows, wide), f32),
            pltpu.VMEM((n, 1, wide), f32),
            pltpu.VMEM((n, 1, wide), f32),
            pltpu.VMEM((n, rows, wide), bf16),
            pltpu.VMEM((n, rows, wide), bf16),
            pltpu.VMEM((n, rows, depth), bf16),
            pltpu.VMEM((n, rows, depth), bf16),
            pltpu.VMEM((n, rows, depth), bf16),
            pltpu.VMEM((n, rows, depth), bf16),
            pltpu.SemaphoreType.DMA((4,)),
        ]
        + [dma] * 8,
        compiler_params=pltpu.CompilerParams(
            collective_id=0, has_side_effects=True, vmem_limit_bytes=56 * 2**20
        ),
    )(block_order, query, keys, values, ratio)


def solution(mesh):
    spec = P("head", ("groups", "seq"), None)
    return jax.shard_map(
        functools.partial(body, mesh.shape["seq"]),
        mesh=mesh,
        in_specs=(spec, spec, spec, spec, P("groups")),
        out_specs=(spec, spec, spec),
        check_vma=False,
    )
```

```python
import functools
import math

import jax
import jax.numpy as jnp
from jax import lax
from jax.experimental import pallas as pl
from jax.experimental.pallas import tpu as pltpu
from jax.sharding import PartitionSpec as P

MESH = pl.DeviceIdType.MESH
MASKED = -1e30
NT = (((1,), (1,)), ((), ()))
TN = (((0,), (0,)), ((), ()))


def dot(a, b, dims=None):
    if dims is None:
        return jnp.dot(a, b, preferred_element_type=jnp.float32)
    return lax.dot_general(a, b, dims, preferred_element_type=jnp.float32)


def each(first, last, step):
    if last - first <= 8:
        for i in range(first, last):
            step(i)
    else:
        pl.loop(first, last)(step)


def kernel(
    n,
    order_ref,
    query_hbm,
    keys_hbm,
    values_hbm,
    ratio_hbm,
    query_rel,
    sides,
    query,
    ratio,
    kbuf,
    vbuf,
    exps,
    grads,
    tops,
    sums,
    parts,
    low,
    soft,
    dv_out,
    dk_out,
    dv_in,
    dk_in,
    local_sem,
    k_send,
    k_recv,
    v_send,
    v_recv,
    dv_send,
    dv_recv,
    dk_send,
    dk_recv,
):
    heads, rows, depth = query_hbm.shape
    wide = heads * rows
    scale = depth**-0.5
    rate = scale * math.log2(math.e)
    per_device = order_ref.shape[0] // n
    block_rows = rows // per_device
    me = lax.axis_index("seq")

    pair = me + 1 - 2 * lax.rem(me, 2)

    def peer(d, sign):
        odd = d % 2
        return lax.rem(me + (pair - me) * odd + n + sign * (d - odd), n)

    def to(d):
        return {"seq": peer(d, 1)}

    def back(d):
        return {"seq": peer(d, -1)}

    def each_peer(step):
        each(2, n, step)
        step(1)

    loads = [
        pltpu.make_async_copy(keys_hbm.at[0], kbuf.at[0], local_sem.at[0]),
        pltpu.make_async_copy(query_hbm, query, local_sem.at[1]),
        pltpu.make_async_copy(ratio_hbm, ratio, local_sem.at[2]),
        pltpu.make_async_copy(values_hbm.at[0], vbuf.at[0], local_sem.at[3]),
    ]
    for load in loads:
        load.start()

    barrier = pltpu.get_barrier_semaphore()

    def greet(d):
        pl.semaphore_signal(barrier, inc=1, device_id=to(d), device_id_type=MESH)

    each(1, n, greet)
    pl.semaphore_wait(barrier, n - 1)

    def k_copy(d):
        return pltpu.make_async_remote_copy(
            src_ref=keys_hbm.at[0],
            dst_ref=kbuf.at[d],
            send_sem=k_send.at[d],
            recv_sem=k_recv.at[d],
            device_id=to(d),
            device_id_type=MESH,
        )

    def v_copy(d):
        return pltpu.make_async_remote_copy(
            src_ref=values_hbm.at[0],
            dst_ref=vbuf.at[d],
            send_sem=v_send.at[d],
            recv_sem=v_recv.at[d],
            device_id=to(d),
            device_id_type=MESH,
        )

    def dv_copy(d):
        return pltpu.make_async_remote_copy(
            src_ref=dv_out.at[d],
            dst_ref=dv_in.at[d],
            send_sem=dv_send.at[d],
            recv_sem=dv_recv.at[d],
            device_id=back(d),
            device_id_type=MESH,
        )

    def dk_copy(d):
        return pltpu.make_async_remote_copy(
            src_ref=dk_out.at[d],
            dst_ref=dk_in.at[d],
            send_sem=dk_send.at[d],
            recv_sem=dk_recv.at[d],
            device_id=back(d),
            device_id_type=MESH,
        )

    each_peer(lambda d: k_copy(d).start())
    each_peer(lambda d: v_copy(d).start())

    def places(owner, axis):
        index = lax.broadcasted_iota(jnp.int32, (rows, rows), axis)
        within = lax.rem(index, block_rows)
        first = order_ref[owner * per_device] * block_rows
        for b in range(1, per_device):
            first = jnp.where(
                index >= b * block_rows, order_ref[owner * per_device + b] * block_rows, first
            )
        return first + within

    loads[0].wait()
    loads[1].wait()
    query_places = places(me, 1)

    def score_step(d):
        owner = peer(d, -1)
        bias = jnp.where(places(owner, 0) <= query_places, 0.0, MASKED)
        rows_in = query[...].reshape(wide, depth)
        scores = dot(kbuf[d], rows_in, NT) + jnp.concatenate([bias] * heads, axis=1)
        top = jnp.max(scores, axis=0, keepdims=True)
        e = jnp.exp2((scores - top) * rate)
        exps[d] = e
        tops[d] = top
        sums[d] = jnp.sum(e, axis=0, keepdims=True)

    score_step(0)
    loads[2].wait()
    loads[3].wait()

    def grad_step(d):
        grads[d] = dot(vbuf[d], ratio[...].reshape(wide, depth), NT)

    grad_step(0)

    def expect_step(d):
        parts[d] = jnp.sum(exps[d] * grads[d], axis=0, keepdims=True)

    def k_step(d):
        k_copy(d).wait_recv()
        score_step(d)

    each(1, n, k_step)

    top = jnp.max(tops[...], axis=0)
    total = jnp.sum(sums[...] * jnp.exp2((tops[...] - top) * rate), axis=0)
    inverse = 1.0 / total

    def weight_step(d):
        w = exps[d] * (jnp.exp2((tops[d] - top) * rate) * inverse)
        exps[d] = w
        low[d] = w.astype(jnp.bfloat16)

    def value_part(d):
        return dot(low[d], ratio[...].reshape(wide, depth))

    def dv_step(d):
        weight_step(d)
        dv_out[d] = value_part(d).astype(jnp.bfloat16)
        dv_copy(d).start()

    each(1, n, dv_step)
    weight_step(0)
    own_value = value_part(0)
    expect_step(0)

    def v_step(d):
        v_copy(d).wait_recv()
        grad_step(d)
        expect_step(d)

    each(1, n, v_step)

    expect = jnp.sum(parts[...], axis=0)

    def soft_step(d):
        soft[d] = (exps[d] * (grads[d] - expect)).astype(jnp.bfloat16)

    def key_part(d):
        return dot(soft[d], query[...].reshape(wide, depth))

    def dk_step(d):
        soft_step(d)
        dk_out[d] = key_part(d).astype(jnp.bfloat16)
        dk_copy(d).start()

    each_peer(dk_step)
    soft_step(0)
    own_key = key_part(0)

    query_sum = dot(
        kbuf[...].reshape(n * rows, depth), soft[...].reshape(n * rows, wide), TN
    )
    for h in range(heads):
        query_rel[h] = (
            0.5
            * scale
            * query[h].astype(jnp.float32)
            * query_sum[:, h * rows : (h + 1) * rows].T
        )

    each(1, n, lambda d: dv_copy(d).wait_recv())
    sides[1] = vbuf[0].astype(jnp.float32) * (
        own_value + jnp.sum(dv_in[1:].astype(jnp.float32), axis=0)
    )
    each(1, n, lambda d: dk_copy(d).wait_recv())
    sides[0] = (
        0.5
        * scale
        * kbuf[0].astype(jnp.float32)
        * (own_key + jnp.sum(dk_in[1:].astype(jnp.float32), axis=0))
    )

    def drain(d):
        k_copy(d).wait_send()
        v_copy(d).wait_send()
        dv_copy(d).wait_send()
        dk_copy(d).wait_send()

    each(1, n, drain)


def body(n, query, keys, values, ratio, block_order):
    heads, rows, depth = query.shape
    wide = heads * rows
    bf16, f32 = jnp.bfloat16, jnp.float32
    anywhere = pl.BlockSpec(memory_space=pl.ANY)
    vmem = pl.BlockSpec(memory_space=pltpu.VMEM)
    dma = pltpu.SemaphoreType.DMA((n,))
    query_rel, sides = pl.pallas_call(
        functools.partial(kernel, n),
        out_shape=[
            pltpu.VMEM(query.shape, f32),
            pltpu.VMEM((2,) + keys.shape[1:], f32),
        ],
        in_specs=[pl.BlockSpec(memory_space=pltpu.SMEM)] + [anywhere] * 4,
        out_specs=[vmem] * 2,
        scratch_shapes=[
            pltpu.VMEM((heads, rows, depth), bf16),
            pltpu.VMEM((heads, rows, depth), bf16),
            pltpu.VMEM((n, rows, depth), bf16),
            pltpu.VMEM((n, rows, depth), bf16),
            pltpu.VMEM((n, rows, wide), f32),
            pltpu.VMEM((n, rows, wide), f32),
            pltpu.VMEM((n, 1, wide), f32),
            pltpu.VMEM((n, 1, wide), f32),
            pltpu.VMEM((n, 1, wide), f32),
            pltpu.VMEM((n, rows, wide), bf16),
            pltpu.VMEM((n, rows, wide), bf16),
            pltpu.VMEM((n, rows, depth), bf16),
            pltpu.VMEM((n, rows, depth), bf16),
            pltpu.VMEM((n, rows, depth), bf16),
            pltpu.VMEM((n, rows, depth), bf16),
            pltpu.SemaphoreType.DMA((4,)),
        ]
        + [dma] * 8,
        compiler_params=pltpu.CompilerParams(
            collective_id=0, has_side_effects=True, vmem_limit_bytes=56 * 2**20
        ),
    )(block_order, query, keys, values, ratio)
    return query_rel, sides[:1], sides[1:]


def solution(mesh):
    spec = P("head", ("groups", "seq"), None)
    return jax.shard_map(
        functools.partial(body, mesh.shape["seq"]),
        mesh=mesh,
        in_specs=(spec, spec, spec, spec, P("groups")),
        out_specs=(spec, spec, spec),
        check_vma=False,
    )
```

```python
import functools
import math

import jax
import jax.numpy as jnp
from jax import lax
from jax.experimental import pallas as pl
from jax.experimental.pallas import tpu as pltpu
from jax.sharding import PartitionSpec as P

MESH = pl.DeviceIdType.MESH
MASKED = -1e30
NT = (((1,), (1,)), ((), ()))
TN = (((0,), (0,)), ((), ()))


def dot(a, b, dims=None):
    if dims is None:
        return jnp.dot(a, b, preferred_element_type=jnp.float32)
    return lax.dot_general(a, b, dims, preferred_element_type=jnp.float32)


def each(first, last, step):
    if last - first <= 8:
        for i in range(first, last):
            step(i)
    else:
        pl.loop(first, last)(step)


def kernel(
    n,
    order_ref,
    query_hbm,
    keys_hbm,
    values_hbm,
    ratio_hbm,
    query_rel,
    sides,
    query,
    ratio,
    kbuf,
    vbuf,
    exps,
    grads,
    tops,
    sums,
    parts,
    low,
    soft,
    dv_out,
    dk_out,
    dv_in,
    dk_in,
    local_sem,
    k_send,
    k_recv,
    v_send,
    v_recv,
    dv_send,
    dv_recv,
    dk_send,
    dk_recv,
):
    heads, rows, depth = query_hbm.shape
    wide = heads * rows
    scale = depth**-0.5
    rate = scale * math.log2(math.e)
    per_device = order_ref.shape[0] // n
    block_rows = rows // per_device
    me = lax.axis_index("seq")

    pair = me + 1 - 2 * lax.rem(me, 2)

    def peer(d, sign):
        odd = d % 2
        return lax.rem(me + (pair - me) * odd + n + sign * (d - odd), n)

    def to(d):
        return {"seq": peer(d, 1)}

    def back(d):
        return {"seq": peer(d, -1)}

    def each_peer(step):
        each(2, n, step)
        step(1)

    loads = [
        pltpu.make_async_copy(keys_hbm.at[0], kbuf.at[0], local_sem.at[0]),
        pltpu.make_async_copy(query_hbm, query, local_sem.at[1]),
        pltpu.make_async_copy(ratio_hbm, ratio, local_sem.at[2]),
        pltpu.make_async_copy(values_hbm.at[0], vbuf.at[0], local_sem.at[3]),
    ]

    barrier = pltpu.get_barrier_semaphore()

    def greet(d):
        pl.semaphore_signal(barrier, inc=1, device_id=to(d), device_id_type=MESH)

    each(1, n, greet)
    for load in loads:
        load.start()
    pl.semaphore_wait(barrier, n - 1)

    def k_copy(d):
        return pltpu.make_async_remote_copy(
            src_ref=keys_hbm.at[0],
            dst_ref=kbuf.at[d],
            send_sem=k_send.at[d],
            recv_sem=k_recv.at[d],
            device_id=to(d),
            device_id_type=MESH,
        )

    def v_copy(d):
        return pltpu.make_async_remote_copy(
            src_ref=values_hbm.at[0],
            dst_ref=vbuf.at[d],
            send_sem=v_send.at[d],
            recv_sem=v_recv.at[d],
            device_id=to(d),
            device_id_type=MESH,
        )

    def dv_copy(d):
        return pltpu.make_async_remote_copy(
            src_ref=dv_out.at[d],
            dst_ref=dv_in.at[d],
            send_sem=dv_send.at[d],
            recv_sem=dv_recv.at[d],
            device_id=back(d),
            device_id_type=MESH,
        )

    def dk_copy(d):
        return pltpu.make_async_remote_copy(
            src_ref=dk_out.at[d],
            dst_ref=dk_in.at[d],
            send_sem=dk_send.at[d],
            recv_sem=dk_recv.at[d],
            device_id=back(d),
            device_id_type=MESH,
        )

    each_peer(lambda d: k_copy(d).start())
    each(1, n, lambda d: v_copy(d).start())

    def places(owner, axis):
        index = lax.broadcasted_iota(jnp.int32, (rows, rows), axis)
        within = lax.rem(index, block_rows)
        first = order_ref[owner * per_device] * block_rows
        for b in range(1, per_device):
            first = jnp.where(
                index >= b * block_rows, order_ref[owner * per_device + b] * block_rows, first
            )
        return first + within

    loads[0].wait()
    loads[1].wait()
    query_places = places(me, 1)

    def score_step(d):
        owner = peer(d, -1)
        bias = jnp.where(places(owner, 0) <= query_places, 0.0, MASKED)
        rows_in = query[...].reshape(wide, depth)
        scores = dot(kbuf[d], rows_in, NT) + jnp.concatenate([bias] * heads, axis=1)
        top = jnp.max(scores, axis=0, keepdims=True)
        e = jnp.exp2((scores - top) * rate)
        exps[d] = e
        tops[d] = top
        sums[d] = jnp.sum(e, axis=0, keepdims=True)

    score_step(0)
    loads[2].wait()
    loads[3].wait()

    def grad_step(d):
        grads[d] = dot(vbuf[d], ratio[...].reshape(wide, depth), NT)

    grad_step(0)

    def expect_step(d):
        parts[d] = jnp.sum(exps[d] * grads[d], axis=0, keepdims=True)

    def k_step(d):
        k_copy(d).wait_recv()
        score_step(d)

    each(1, n, k_step)

    top = jnp.max(tops[...], axis=0)
    total = jnp.sum(sums[...] * jnp.exp2((tops[...] - top) * rate), axis=0)
    inverse = 1.0 / total

    def weight_step(d):
        w = exps[d] * (jnp.exp2((tops[d] - top) * rate) * inverse)
        exps[d] = w
        low[d] = w.astype(jnp.bfloat16)

    def value_part(d):
        return dot(low[d], ratio[...].reshape(wide, depth))

    def dv_step(d):
        weight_step(d)
        dv_out[d] = value_part(d).astype(jnp.bfloat16)
        dv_copy(d).start()

    each(1, n, dv_step)
    weight_step(0)
    own_value = value_part(0)
    expect_step(0)

    def v_step(d):
        v_copy(d).wait_recv()
        grad_step(d)
        expect_step(d)

    each(1, n, v_step)

    expect = jnp.sum(parts[...], axis=0)

    def soft_step(d):
        soft[d] = (exps[d] * (grads[d] - expect)).astype(jnp.bfloat16)

    def key_part(d):
        return dot(soft[d], query[...].reshape(wide, depth))

    def dk_step(d):
        soft_step(d)
        dk_out[d] = key_part(d).astype(jnp.bfloat16)
        dk_copy(d).start()

    each_peer(dk_step)
    soft_step(0)
    own_key = key_part(0)

    query_sum = dot(
        kbuf[...].reshape(n * rows, depth), soft[...].reshape(n * rows, wide), TN
    )
    for h in range(heads):
        query_rel[h] = (
            0.5
            * scale
            * query[h].astype(jnp.float32)
            * query_sum[:, h * rows : (h + 1) * rows].T
        )

    each(1, n, lambda d: dv_copy(d).wait_recv())
    sides[1] = vbuf[0].astype(jnp.float32) * (
        own_value + jnp.sum(dv_in[1:].astype(jnp.float32), axis=0)
    )
    each(1, n, lambda d: dk_copy(d).wait_recv())
    sides[0] = (
        0.5
        * scale
        * kbuf[0].astype(jnp.float32)
        * (own_key + jnp.sum(dk_in[1:].astype(jnp.float32), axis=0))
    )

    def drain(d):
        k_copy(d).wait_send()
        v_copy(d).wait_send()
        dv_copy(d).wait_send()
        dk_copy(d).wait_send()

    each(1, n, drain)


def body(n, query, keys, values, ratio, block_order):
    heads, rows, depth = query.shape
    wide = heads * rows
    bf16, f32 = jnp.bfloat16, jnp.float32
    anywhere = pl.BlockSpec(memory_space=pl.ANY)
    vmem = pl.BlockSpec(memory_space=pltpu.VMEM)
    dma = pltpu.SemaphoreType.DMA((n,))
    query_rel, sides = pl.pallas_call(
        functools.partial(kernel, n),
        out_shape=[
            pltpu.VMEM(query.shape, f32),
            pltpu.VMEM((2,) + keys.shape[1:], f32),
        ],
        in_specs=[pl.BlockSpec(memory_space=pltpu.SMEM)] + [anywhere] * 4,
        out_specs=[vmem] * 2,
        scratch_shapes=[
            pltpu.VMEM((heads, rows, depth), bf16),
            pltpu.VMEM((heads, rows, depth), bf16),
            pltpu.VMEM((n, rows, depth), bf16),
            pltpu.VMEM((n, rows, depth), bf16),
            pltpu.VMEM((n, rows, wide), f32),
            pltpu.VMEM((n, rows, wide), f32),
            pltpu.VMEM((n, 1, wide), f32),
            pltpu.VMEM((n, 1, wide), f32),
            pltpu.VMEM((n, 1, wide), f32),
            pltpu.VMEM((n, rows, wide), bf16),
            pltpu.VMEM((n, rows, wide), bf16),
            pltpu.VMEM((n, rows, depth), bf16),
            pltpu.VMEM((n, rows, depth), bf16),
            pltpu.VMEM((n, rows, depth), bf16),
            pltpu.VMEM((n, rows, depth), bf16),
            pltpu.SemaphoreType.DMA((4,)),
        ]
        + [dma] * 8,
        compiler_params=pltpu.CompilerParams(
            collective_id=0, has_side_effects=True, vmem_limit_bytes=56 * 2**20
        ),
    )(block_order, query, keys, values, ratio)
    return query_rel, sides[:1], sides[1:]


def solution(mesh):
    spec = P("head", ("groups", "seq"), None)
    return jax.shard_map(
        functools.partial(body, mesh.shape["seq"]),
        mesh=mesh,
        in_specs=(spec, spec, spec, spec, P("groups")),
        out_specs=(spec, spec, spec),
        check_vma=False,
    )
```
